256 devices in a mesh: seq: 64 (over x, y, z_lo, core), state: 4 (over z_hi).
Axes of the slice: x: 4, y: 4, z: 8 (z_hi: 4, z_lo: 2; z = z_hi * 2 + z_lo), core: 2. Of those that a mesh axis runs over, the one named last changes fastest.
Arguments:
- outer_factor: bfloat16 [256, 256, 256], P('state'), may hold values from -0.375 to 0.375
- inner_factor: bfloat16 [256, 256, 256], P('state', 'seq'), may hold values from -0.375 to 0.375
- alpha_start: bfloat16 [256, 65536], P('seq', 'state'), may hold values from -16 to 16
- beta_end: bfloat16 [256, 65536], P('seq', 'state'), may hold values from -6 to 6
- emissions: bfloat16 [4, 256, 65536], P(None, 'seq', 'state'), may hold values from 0.5 to 2
- normalizers: float32 [4, 256], P(None, 'seq'), may hold values from 0.7 to 2
Outputs:
- beta_start: float32 [256, 65536], P('seq', 'state')
- inner_grad: float32 [256, 256, 256], P('state', 'seq')
The draws below stay inside these ranges and needn't reach their ends.
All inputs are finite; a program needn't handle non-finite values.
Results may differ from the reference program's by a relative error of at most 0.015.
Values may be sent and summed in bfloat16 or wider, within the bound.
A program may use at most 192 MiB of HBM per device.

```python
import math
import jax
import jax.numpy as jnp

BLK = 256
STATES = 65536
STEPS = 4
SEQS = 256


def strengthened(entries, key, source, target, parts, factor):
    owner, partner = [(jnp.arange(entries.shape[axis_at]) // (entries.shape[axis_at] // parts)).reshape([-1 if axis == axis_at else 1 for axis in range(entries.ndim)]) for axis_at in (source, target)]
    chosen = jax.random.permutation(key, parts)[partner]
    strong = (owner == chosen) | (owner == (partner + parts // 2) % parts)
    return jnp.where(strong, factor * entries, entries)


def shard_levels(key, shape, cuts, smallest, largest):
    def one(dim, blocks):
        steps = jax.random.uniform(jax.random.fold_in(jax.random.fold_in(key, 6), dim), (blocks,), jnp.float32, smallest / len(cuts), largest / len(cuts))
        return jnp.repeat(jnp.exp(steps), shape[dim] // blocks).reshape((-1,) + (1,) * (len(shape) - dim - 1))

    loudness = one(*cuts[0])
    for cut in cuts[1:]:
        loudness = loudness * one(*cut)
    return loudness


def scatter_about(stream_key, extent, scale, most, split=(), held_as=jnp.bfloat16):
    drawn = jax.random.normal(stream_key, extent, jnp.float32) * scale
    if len(split) > 0:
        drawn = shard_levels(stream_key, extent, split, -0.22, 0.18) * drawn
    return jnp.clip(drawn, min=-most, max=most).astype(held_as)


def gaussian_with(key, shape, width, most, pieces, heavy, held_as=jnp.bfloat16):
    result = width * jax.random.normal(key, shape, jnp.float32)
    if pieces:
        result = result * shard_levels(key, shape, pieces, -0.22, 0.18)
    return jnp.clip(strengthened(result, jax.random.fold_in(key, 3), *heavy), -most, most).astype(held_as)


def setup_inputs(seed: int = 0) -> dict:
    splits = jax.random.split(jax.random.key(seed), 7)
    return {
        "outer_factor": scatter_about(splits[0], (BLK, BLK, BLK), BLK ** -0.5, 0.375, ((0, 4),)),
        "inner_factor": scatter_about(splits[1], (BLK, BLK, BLK), BLK ** -0.5, 0.375, ((0, 4), (1, 64))),
        "alpha_start": gaussian_with(splits[2], (SEQS, STATES), 1.0, 16.0, ((0, 64), (1, 4)), (0, 1, 64, 4.0)),
        "beta_end": scatter_about(splits[3], (SEQS, STATES), 1.0, 6.0, ((0, 64), (1, 4))),
        "emissions": jnp.clip(jnp.exp(math.log(2.0) - 1.3862944 * jax.random.uniform(splits[4], (STEPS, SEQS, STATES), jnp.float32) ** shard_levels(splits[4], (STEPS, SEQS, STATES), ((1, 64), (2, 4)), -0.2, 0.2)), 0.5, 2.0).astype(jnp.bfloat16),
        "normalizers": jnp.clip(jnp.exp(math.log(2.0) - 1.0498221 * jax.random.uniform(splits[5], (STEPS, SEQS), jnp.float32) ** shard_levels(splits[5], (STEPS, SEQS), ((1, 64),), -0.2, 0.2)), 0.7, 2.0),
    }


def reference(outer_factor, inner_factor, alpha_start, beta_end, emissions, normalizers):
    seq_count = alpha_start.shape[0]
    step_count = emissions.shape[0]
    block_size = outer_factor.shape[0]
    outer_full = outer_factor.astype(jnp.float32)
    inner_full = inner_factor.astype(jnp.float32)

    def as_blocks(flat):
        return flat.reshape(seq_count, block_size, block_size)
    forward_msg = as_blocks(alpha_start)
    inner_inputs = []
    for step_index in range(step_count):
        mixed = jnp.einsum('nki,kij->nkj', forward_msg.astype(jnp.float32), outer_full).astype(jnp.bfloat16)
        inner_in = jnp.swapaxes(mixed, 1, 2)
        inner_inputs.append(inner_in)
        if step_index + 1 < step_count:
            lifted = jnp.einsum('nja,jab->njb', inner_in.astype(jnp.float32), inner_full).astype(jnp.bfloat16)
            scaled = jnp.swapaxes(lifted, 1, 2).astype(jnp.float32) * as_blocks(emissions[step_index]).astype(jnp.float32)
            forward_msg = (scaled / normalizers[step_index][:, None, None]).astype(jnp.bfloat16)
    backward_msg = as_blocks(beta_end).astype(jnp.float32)
    gradient = jnp.zeros((block_size, block_size, block_size), jnp.float32)
    for step_index in reversed(range(step_count)):
        scaled = as_blocks(emissions[step_index]).astype(jnp.float32) * backward_msg
        weighted = (scaled / normalizers[step_index][:, None, None]).astype(jnp.bfloat16)
        inner_out = jnp.swapaxes(weighted, 1, 2)
        pushed = jnp.einsum('njb,jab->nja', inner_out.astype(jnp.float32), inner_full).astype(jnp.bfloat16)
        backward_msg = jnp.einsum('nkj,kij->nki', jnp.swapaxes(pushed, 1, 2).astype(jnp.float32), outer_full)
        gradient = gradient + jnp.einsum('nja,njb->jab', inner_inputs[step_index].astype(jnp.float32), inner_out.astype(jnp.float32))
    grad_scale = 1.0 / math.sqrt(seq_count * step_count)
    return (backward_msg.reshape(seq_count, -1), gradient * grad_scale)
```

```python
import functools

import jax
import jax.numpy as jnp
from jax import lax
from jax.experimental import pallas as pl
from jax.experimental.pallas import tpu as pltpu
from jax.sharding import PartitionSpec as P

MESH = pl.DeviceIdType.MESH
F32, BF16 = jnp.float32, jnp.bfloat16

GROUP = 8
PEERS = 32
SEQ = 64
STEPS = 4


def iota(shape, dim):
    return lax.broadcasted_iota(jnp.int32, shape, dim)


def kernel(
    norm_ref, outer_hbm, inner_ref, alpha_ref, beta_ref, emis_ref,
    beta_out, grad_out,
    outer_nat, outer_tr, inner_nat, inner_tr, gathered, sent, received, grad_sent, grad_received,
    ins_tr, outs, rows_in, rows_out,
    load_sem, send_sem, recv_sem, gather_send, gather_recv, grad_send, grad_recv,
):
    seq, state = lax.axis_index("seq"), lax.axis_index("state")
    x = lax.div(seq, 16)
    y = lax.rem(lax.div(seq, 4), 4)
    low = lax.rem(lax.div(seq, 2), 2)
    core = lax.rem(seq, 2)
    place = y * 2 + core
    me = state * GROUP + place

    load = pltpu.make_async_copy(outer_hbm, outer_nat, load_sem)
    load.start()

    xs = [lax.rem(x + d, 4) for d in range(4)]
    ys = [lax.rem(y + d, 4) for d in range(4)]
    lows = [low, 1 - low]
    cores = [core, 1 - core]
    states = [lax.rem(state + d, 4) for d in range(4)]
    far = (2, 1, 3, 0)
    peers = [
        (states[ds] * GROUP + ys[dy] * 2 + cores[dc], x * 16 + ys[dy] * 4 + low * 2 + cores[dc], states[ds], ds)
        for ds in far for dy in far for dc in (1, 0) if ds or dy or dc
    ]
    mates = [
        (xs[dx] * 16 + ys[dy] * 4 + lows[dl] * 2 + cores[dc], ys[dy] * 2 + cores[dc], dx)
        for dx in far for dy in far for dl in (1, 0) for dc in (1, 0) if dx or dy or dl or dc
    ]

    barrier = pltpu.get_barrier_semaphore()
    greeted = 0
    for _, to_seq, to_state, ds in peers:
        if ds:
            pl.semaphore_signal(barrier, 1, device_id=(to_seq, to_state), device_id_type=MESH)
            greeted += 1
    for to_seq, _, _ in mates:
        pl.semaphore_signal(barrier, 1, device_id=(to_seq, state), device_id_type=MESH)
        greeted += 1

    def send(slot):
        for to, to_seq, to_state, _ in peers:
            pltpu.make_async_remote_copy(
                src_ref=sent.at[slot, to],
                dst_ref=received.at[slot, me],
                send_sem=send_sem.at[slot],
                recv_sem=recv_sem.at[slot],
                device_id=(to_seq, to_state),
                device_id_type=MESH,
            ).start()
        received[slot, pl.ds(me, 1)] = sent[slot, pl.ds(me, 1)]

    def wait(slot):
        others = received.at[slot, pl.ds(0, PEERS - 1)]
        pltpu.make_async_copy(others, others, recv_sem.at[slot]).wait()

    low_half = iota((128, 128), 1) < 64

    def swap(a):
        return pltpu.roll(a, 64, 1)

    def at_inner(slot):
        a = [received[slot, s * GROUP : (s + 1) * GROUP].astype(F32).reshape(128, 128) for s in range(4)]
        top = [jnp.where(low_half, a[0], swap(a[1])), jnp.where(low_half, a[2], swap(a[3]))]
        bottom = [jnp.where(low_half, swap(a[0]), a[1]), jnp.where(low_half, swap(a[2]), a[3])]
        return jnp.concatenate([jnp.concatenate(top, axis=1), jnp.concatenate(bottom, axis=1)], axis=0)

    def from_inner(o, slot):
        for u in range(2):
            even, odd = o[:128, u * 128 : (u + 1) * 128], o[128:, u * 128 : (u + 1) * 128]
            first = jnp.where(low_half, even, swap(odd))
            second = jnp.where(low_half, swap(even), odd)
            sent[slot, 2 * u * GROUP : (2 * u + 1) * GROUP] = first.astype(BF16).reshape(GROUP, 16, 128)
            sent[slot, (2 * u + 1) * GROUP : (2 * u + 2) * GROUP] = second.astype(BF16).reshape(GROUP, 16, 128)

    def through_inner(a, factor):
        block = lax.rem(iota((256, 256), 0), 8)
        spread = jnp.concatenate([jnp.where(block == b, a, 0.0).astype(BF16) for b in range(8)], axis=1)
        return jnp.dot(spread, factor[...], preferred_element_type=F32)

    def at_outer(slot):
        a = received[slot].astype(F32)
        both = jnp.concatenate([a[:, :8].reshape(256, 128), a[:, 8:].reshape(256, 128)], axis=1)
        return both.T

    def from_outer(a, slot):
        t = a.T.reshape(PEERS, 8, 256)
        sent[slot] = jnp.concatenate([t[:, :, :128], t[:, :, 128:]], axis=1).astype(BF16)

    def through_outer(a, factor):
        rows_in[...] = a

        def sixteen(g, carry):
            parts = [rows_in[pl.ds(pl.multiple_of(n * 64 + g * 16, 16), 16), :] for n in range(4)]
            part = jnp.concatenate(parts, axis=0)
            block = lax.rem(iota((64, 256), 0), 16)
            spread = jnp.concatenate([jnp.where(block == b, part, 0.0).astype(BF16) for b in range(16)], axis=1)
            o = jnp.dot(
                spread, factor[pl.ds(pl.multiple_of(g * 4096, 4096), 4096), :], preferred_element_type=F32
            )
            for n in range(4):
                rows_out[pl.ds(pl.multiple_of(n * 64 + g * 16, 16), 16), :] = o[n * 16 : (n + 1) * 16]
            return carry

        lax.fori_loop(0, 4, sixteen, 0)
        return rows_out[...]

    def reweight(a, step):
        scaled = a * emis_ref[step].astype(F32)
        return jnp.concatenate(
            [scaled[n * 64 : (n + 1) * 64] / jnp.full((64, 256), norm_ref[step, n], F32) for n in range(4)], axis=0
        )

    def regroup(transposed):
        r, c = iota((512, 512), 1 if transposed else 0), iota((512, 512), 0 if transposed else 1)
        return jnp.where(c == (r // 4) % 16 * 32 + r // 64 * 4 + r % 4, 1.0, 0.0).astype(BF16)

    from_outer(reweight(beta_ref[...].astype(F32), STEPS - 1), 0)
    pl.semaphore_wait(barrier, greeted)
    send(0)
    for to_seq, to_place, _ in mates:
        pltpu.make_async_remote_copy(
            src_ref=inner_ref.at[to_place],
            dst_ref=gathered.at[seq],
            send_sem=gather_send,
            recv_sem=gather_recv,
            device_id=(to_seq, state),
            device_id_type=MESH,
        ).start()
    gathered[pl.ds(seq, 1)] = inner_ref[pl.ds(place, 1)]

    load.wait()
    from_outer(through_outer(alpha_ref[...].astype(F32), outer_nat), 8)
    send(8)

    def turn(k, carry):
        at = pl.ds(pl.multiple_of(k * 256, 256), 256)
        outer_tr[at, :] = outer_nat[at, :].T
        return carry

    lax.fori_loop(0, 64, turn, 0)

    def wait_mates(ref, sem):
        others = ref.at[pl.ds(0, SEQ - 1)]
        pltpu.make_async_copy(others, others, sem).wait()

    wait_mates(gathered, gather_recv)
    move = regroup(False)
    for c in range(4):
        o = jnp.dot(move, gathered[c * 16 : (c + 1) * 16].reshape(512, 256), preferred_element_type=F32)
        for b in range(8):
            inner_nat[b * 256 + c * 64 : b * 256 + (c + 1) * 64, :] = o[b * 64 : (b + 1) * 64].astype(BF16)
    for b in range(8):
        inner_tr[b * 256 : (b + 1) * 256, :] = inner_nat[b * 256 : (b + 1) * 256, :].T

    def backward_inner(t):
        wait(t)
        a = at_inner(t)
        outs[STEPS - 1 - t] = a.astype(BF16)
        from_inner(through_inner(a, inner_tr), 4 + t)
        send(4 + t)

    def forward_arrives(t):
        wait(8 + t)
        a = at_inner(8 + t)
        ins_tr[t] = a.T.astype(BF16)
        return a

    def step(t, carry):
        backward_inner(t)
        from_inner(through_inner(forward_arrives(t), inner_nat), 12 + t)
        send(12 + t)
        wait(4 + t)
        from_outer(reweight(through_outer(at_outer(4 + t), outer_tr), STEPS - 2 - t), t + 1)
        send(t + 1)
        wait(12 + t)
        from_outer(through_outer(reweight(at_outer(12 + t), t), outer_nat), 9 + t)
        send(9 + t)
        return carry

    lax.fori_loop(0, STEPS - 1, step, 0)

    backward_inner(STEPS - 1)
    forward_arrives(STEPS - 1)

    move_back = regroup(True)
    lane_block = lax.rem(iota((64, 256), 1), 8)
    for dx in far:
        c = xs[dx]
        spread = []
        for t in range(STEPS):
            part = ins_tr[t, pl.ds(pl.multiple_of(c * 64, 64), 64), :].astype(F32)
            spread.append(
                jnp.concatenate([jnp.where(lane_block == b, part, 0.0).astype(BF16) for b in range(8)], axis=0)
            )
        g = jnp.dot(jnp.concatenate(spread, axis=1), outs[...].reshape(STEPS * 256, 256), preferred_element_type=F32)
        g = jnp.dot(move_back, g.astype(BF16), preferred_element_type=F32).astype(BF16)
        grad_sent[pl.ds(pl.multiple_of(c * 16, 16), 16)] = g.reshape(16, 32, 256)
        for to_seq, _, to_dx in mates:
            if to_dx == dx:
                pltpu.make_async_remote_copy(
                    src_ref=grad_sent.at[to_seq],
                    dst_ref=grad_received.at[seq],
                    send_sem=grad_send,
                    recv_sem=grad_recv,
                    device_id=(to_seq, state),
                    device_id_type=MESH,
                ).start()
    grad_received[pl.ds(seq, 1)] = grad_sent[pl.ds(seq, 1)]

    wait(STEPS + 3)
    beta_out[...] = through_outer(at_outer(STEPS + 3), outer_tr)

    wait_mates(grad_received, grad_recv)
    for q in range(GROUP):
        total = None
        for xx in range(4):
            for ll in range(2):
                share = grad_received[xx * 16 + q // 2 * 4 + ll * 2 + q % 2].astype(F32)
                total = share if total is None else total + share
        grad_out[q * 32 : (q + 1) * 32, :] = total * (1.0 / 32.0)

    for slot in range(15):
        others = sent.at[slot, pl.ds(0, PEERS - 1)]
        pltpu.make_async_copy(others, others, send_sem.at[slot]).wait()
    wait_mates(gathered, gather_send)
    wait_mates(grad_sent, grad_send)


def local(outer_factor, inner_factor, alpha_start, beta_end, emissions, normalizers):
    vmem, hbm = pl.BlockSpec(memory_space=pltpu.VMEM), pl.BlockSpec(memory_space=pl.ANY)
    beta_start, grad = pl.pallas_call(
        kernel,
        out_shape=(jax.ShapeDtypeStruct((256, 256), F32), jax.ShapeDtypeStruct((256, 256), F32)),
        in_specs=[pl.BlockSpec(memory_space=pltpu.SMEM), hbm, vmem, vmem, vmem, vmem],
        out_specs=(vmem, vmem),
        scratch_shapes=[
            pltpu.VMEM((64 * 256, 256), BF16),
            pltpu.VMEM((64 * 256, 256), BF16),
            pltpu.VMEM((8 * 256, 256), BF16),
            pltpu.VMEM((8 * 256, 256), BF16),
            pltpu.VMEM((SEQ, 32, 256), BF16),
            pltpu.VMEM((15, PEERS, 16, 128), BF16),
            pltpu.VMEM((15, PEERS, 16, 128), BF16),
            pltpu.VMEM((SEQ, 32, 256), BF16),
            pltpu.VMEM((SEQ, 32, 256), BF16),
            pltpu.VMEM((STEPS, 256, 256), BF16),
            pltpu.VMEM((STEPS, 256, 256), BF16),
            pltpu.VMEM((256, 256), F32),
            pltpu.VMEM((256, 256), F32),
            pltpu.SemaphoreType.DMA,
            pltpu.SemaphoreType.DMA((15,)),
            pltpu.SemaphoreType.DMA((15,)),
            pltpu.SemaphoreType.DMA,
            pltpu.SemaphoreType.DMA,
            pltpu.SemaphoreType.DMA,
            pltpu.SemaphoreType.DMA,
        ],
        compiler_params=pltpu.CompilerParams(
            collective_id=0, has_side_effects=True, vmem_limit_bytes=56 * 1024 * 1024
        ),
    )(
        normalizers,
        outer_factor.reshape(64 * 256, 256),
        inner_factor.reshape(GROUP, 32, 256),
        alpha_start.reshape(256, 256),
        beta_end.reshape(256, 256),
        emissions.reshape(STEPS, 256, 256),
    )
    return beta_start.reshape(alpha_start.shape), grad.reshape(inner_factor.shape)


def solution(mesh):
    placed = (
        P("state", None, None),
        P("state", "seq", None),
        P("seq", "state"),
        P("seq", "state"),
        P(None, "seq", "state"),
        P(None, "seq"),
    )
    return jax.shard_map(
        local,
        mesh=mesh,
        in_specs=placed,
        out_specs=(P("seq", "state"), P("state", "seq", None)),
        check_vma=False,
    )
```

```python
import functools

import jax
import jax.numpy as jnp
from jax import lax
from jax.experimental import pallas as pl
from jax.experimental.pallas import tpu as pltpu
from jax.sharding import PartitionSpec as P

MESH = pl.DeviceIdType.MESH
F32, BF16 = jnp.float32, jnp.bfloat16

GROUP = 8
PEERS = 32
SEQ = 64
STEPS = 4


def iota(shape, dim):
    return lax.broadcasted_iota(jnp.int32, shape, dim)


def kernel(
    norm_ref, outer_hbm, inner_ref, alpha_ref, beta_ref, emis_ref,
    beta_out, grad_out,
    outer_nat, outer_tr, inner_nat, inner_tr, slab, relay, gathered, sent, received, rows_sent, rows_received,
    grad_sent, emis, rows_in, rows_out, mixed,
    load_sem, send_sem, recv_sem, relay_send, relay_recv, gather_send, gather_recv, core_send, core_recv,
    rows_send, rows_recv, grad_send, grad_recv, grad_own,
):
    seq, state = lax.axis_index("seq"), lax.axis_index("state")
    x = lax.div(seq, 16)
    y = lax.rem(lax.div(seq, 4), 4)
    low = lax.rem(lax.div(seq, 2), 2)
    core = lax.rem(seq, 2)
    place = y * 2 + low
    share = x * 2 + core
    me = state * GROUP + place

    load = pltpu.make_async_copy(outer_hbm, outer_nat, load_sem)
    load.start()

    def hops(d, n):
        return min(d, n - d)

    xs = [lax.rem(x + d, 4) for d in range(4)]
    ys = [lax.rem(y + d, 4) for d in range(4)]
    lows = [low, 1 - low]
    cores = [core, 1 - core]
    zs = [lax.rem(state * 2 + low + d, 8) for d in range(8)]
    far = (2, 1, 3, 0)
    peers = []
    for dz in sorted(range(8), key=lambda d: -hops(d, 8)):
        for dy in far:
            if dz or dy:
                to_state, to_low = lax.div(zs[dz], 2), lax.rem(zs[dz], 2)
                to_place = ys[dy] * 2 + to_low
                peers.append((to_state * GROUP + to_place, x * 16 + ys[dy] * 4 + to_low * 2 + core, to_state))
    mates = [
        xs[dx] * 16 + ys[dy] * 4 + lows[dl] * 2 + cores[dc]
        for dx in far for dy in far for dl in (1, 0) for dc in (1, 0) if dx or dy or dl or dc
    ]
    sharers = [
        (xs[dx] * 2 + cores[dc], xs[dx] * 16 + y * 4 + low * 2 + cores[dc])
        for dx in far for dc in (1, 0) if dx or dc
    ]
    plane = [
        (ys[dy], xs[dx] * 16 + ys[dy] * 4 + low * 2 + core) for dx in far for dy in far if dx or dy
    ]
    beside = x * 16 + y * 4 + (1 - low) * 2 + core
    sibling = x * 16 + y * 4 + low * 2 + 1 - core

    barrier = pltpu.get_barrier_semaphore()
    for dz in range(8):
        for dy in range(4):
            to_state, to_low = lax.div(zs[dz], 2), lax.rem(zs[dz], 2)
            if dz >= 2 and dz <= 6:
                to_seq = x * 16 + ys[dy] * 4 + to_low * 2 + core
                pl.semaphore_signal(barrier, 1, device_id=(to_seq, to_state), device_id_type=MESH)
    to_z = lax.rem(state * 2 + low + jnp.where(low == 0, 7, 1), 8)
    for dy in range(4):
        to_seq = x * 16 + ys[dy] * 4 + lax.rem(to_z, 2) * 2 + core
        pl.semaphore_signal(barrier, 1, device_id=(to_seq, lax.div(to_z, 2)), device_id_type=MESH)
    for to_seq in mates:
        pl.semaphore_signal(barrier, 1, device_id=(to_seq, state), device_id_type=MESH)
    greeted = 5 * 4 + 4 + len(mates)

    def copy(src, dst, send_to, recv_on, to_seq, to_state=state):
        pltpu.make_async_remote_copy(
            src_ref=src, dst_ref=dst, send_sem=send_to, recv_sem=recv_on,
            device_id=(to_seq, to_state), device_id_type=MESH,
        ).start()

    def wait_bytes(ref, sem):
        pltpu.make_async_copy(ref, ref, sem).wait()

    def send(slot):
        for to, to_seq, to_state in peers:
            copy(sent.at[slot, to], received.at[slot, me], send_sem.at[slot], recv_sem.at[slot], to_seq, to_state)
        received[slot, pl.ds(me, 1)] = sent[slot, pl.ds(me, 1)]

    def wait(slot):
        wait_bytes(received.at[slot, pl.ds(0, PEERS - 1)], recv_sem.at[slot])

    def whole(ref, rows=slice(None)):
        return jnp.concatenate([ref[0, rows, :], ref[1, rows, :]], axis=1)

    def put(ref, a, rows=slice(None)):
        ref[0, rows, :] = a[:, :128]
        ref[1, rows, :] = a[:, 128:]

    low_half = iota((128, 128), 1) < 64

    def swap(a):
        return pltpu.roll(a, 64, 1)

    def at_inner(slot):
        a = [received[slot, s * GROUP : (s + 1) * GROUP].astype(F32).reshape(128, 128) for s in range(4)]
        top = [jnp.where(low_half, a[0], swap(a[1])), jnp.where(low_half, a[2], swap(a[3]))]
        bottom = [jnp.where(low_half, swap(a[0]), a[1]), jnp.where(low_half, swap(a[2]), a[3])]
        return jnp.concatenate([jnp.concatenate(top, axis=1), jnp.concatenate(bottom, axis=1)], axis=0)

    def from_inner(o, slot):
        for u in range(2):
            even, odd = o[:128, u * 128 : (u + 1) * 128], o[128:, u * 128 : (u + 1) * 128]
            first = jnp.where(low_half, even, swap(odd))
            second = jnp.where(low_half, swap(even), odd)
            sent[slot, 2 * u * GROUP : (2 * u + 1) * GROUP] = first.astype(BF16).reshape(GROUP, 16, 128)
            sent[slot, (2 * u + 1) * GROUP : (2 * u + 2) * GROUP] = second.astype(BF16).reshape(GROUP, 16, 128)

    def through_inner(a, factor):
        block = lax.rem(iota((256, 256), 0), 8)
        spread = jnp.concatenate([jnp.where(block == b, a, 0.0).astype(BF16) for b in range(8)], axis=1)
        return jnp.dot(spread, factor[...], preferred_element_type=F32)

    def at_outer(slot):
        a = received[slot].astype(F32)
        both = jnp.concatenate([a[:, :8].reshape(256, 128), a[:, 8:].reshape(256, 128)], axis=1)
        return both.T

    def from_outer(a, slot):
        t = a.T.reshape(PEERS, 8, 256)
        sent[slot] = jnp.concatenate([t[:, :, :128], t[:, :, 128:]], axis=1).astype(BF16)

    def through_outer(factor):
        def sixteen(g, carry):
            parts = [whole(rows_in, pl.ds(pl.multiple_of(n * 64 + g * 16, 16), 16)) for n in range(4)]
            part = jnp.concatenate(parts, axis=0)
            block = lax.rem(iota((64, 256), 0), 16)
            spread = jnp.concatenate([jnp.where(block == b, part, 0.0).astype(BF16) for b in range(16)], axis=1)
            o = jnp.dot(
                spread, factor[pl.ds(pl.multiple_of(g * 4096, 4096), 4096), :], preferred_element_type=F32
            )
            for n in range(4):
                put(rows_out, o[n * 16 : (n + 1) * 16], pl.ds(pl.multiple_of(n * 64 + g * 16, 16), 16))
            return carry

        lax.fori_loop(0, 4, sixteen, 0)

    def reweight(a, step):
        scaled = a * whole(emis.at[step])
        return jnp.concatenate(
            [scaled[n * 64 : (n + 1) * 64] / jnp.full((64, 256), norm_ref[step, n], F32) for n in range(4)], axis=0
        )

    def unfold(part, dst):
        def one(k, carry):
            for half in range(2):
                at = pl.ds(pl.multiple_of(k * 256 + half * 128, 128), 128)
                dst[half, pl.ds(k, 4, stride=64), :] = part(at).astype(F32)
            return carry

        lax.fori_loop(0, 64, one, 0, unroll=4)

    def spread_rows(a, slot):
        put(mixed, a)
        for b in range(GROUP):
            rows_sent[slot, b] = whole(mixed, pl.ds(b, 32, stride=8)).astype(BF16)
        for to, to_seq in sharers:
            copy(rows_sent.at[slot, to], rows_received.at[slot, share], rows_send.at[slot], rows_recv.at[slot], to_seq)
        rows_received[slot, pl.ds(share, 1)] = rows_sent[slot, pl.ds(share, 1)]

    for j in range(64):
        put(mixed, inner_ref[j].astype(F32), slice(j * 4, (j + 1) * 4))
    slab[...] = whole(mixed).astype(BF16).reshape(GROUP, 32, 256)
    unfold(lambda at: beta_ref[:, at], rows_out)
    unfold(lambda at: emis_ref[STEPS - 1, :, at], emis.at[STEPS - 1])
    from_outer(reweight(whole(rows_out), STEPS - 1), 0)
    pl.semaphore_wait(barrier, greeted)

    for to_y in range(4):
        copy(slab.at[to_y * 2 + 1 - low], relay.at[to_y], relay_send, relay_recv, beside)
    send(0)
    own, other = low * 2 + core, (1 - low) * 2 + core
    for to_y, to_seq in plane:
        copy(slab.at[to_y * 2 + low], gathered.at[own, x * 4 + y], gather_send.at[0], gather_recv.at[0], to_seq)
    gathered[own, pl.ds(x * 4 + y, 1)] = slab[pl.ds(place, 1)]

    unfold(lambda at: alpha_ref[:, at], rows_in)
    load.wait()
    through_outer(outer_nat)
    from_outer(whole(rows_out), 8)
    send(8)

    wait_bytes(relay, relay_recv)
    for to_y, to_seq in plane:
        copy(relay.at[to_y], gathered.at[other, x * 4 + y], gather_send.at[1], gather_recv.at[1], to_seq)
    gathered[other, pl.ds(x * 4 + y, 1)] = relay[pl.ds(y, 1)]

    def turn(k, carry):
        at = pl.ds(pl.multiple_of(k * 256, 256), 256)
        outer_tr[at, :] = outer_nat[at, :].T
        return carry

    lax.fori_loop(0, 24, turn, 0)
    wait_bytes(gathered.at[own, pl.ds(0, 15)], gather_recv.at[0])
    copy(gathered.at[own], gathered.at[own], core_send.at[0], core_recv.at[0], sibling)
    lax.fori_loop(24, 64, turn, 0)
    wait_bytes(gathered.at[other, pl.ds(0, 15)], gather_recv.at[1])
    copy(gathered.at[other], gathered.at[other], core_send.at[1], core_recv.at[1], sibling)
    for t in range(STEPS - 1):
        unfold(lambda at, t=t: emis_ref[t, :, at], emis.at[t])
    wait_bytes(gathered.at[own], core_recv.at[0])
    wait_bytes(gathered.at[other], core_recv.at[1])

    r, c = iota((512, 512), 0), iota((512, 512), 1)
    move = jnp.where(c == r // 4 % 4 * 128 + r // 16 % 4 * 32 + r // 64 * 4 + r % 4, 1.0, 0.0).astype(BF16)
    for q in range(4):
        part = jnp.concatenate([gathered[lc, q * 4 : (q + 1) * 4].reshape(128, 256) for lc in range(4)], axis=0)
        o = jnp.dot(move, part, preferred_element_type=F32)
        for b in range(8):
            inner_nat[b * 256 + q * 64 : b * 256 + (q + 1) * 64, :] = o[b * 64 : (b + 1) * 64].astype(BF16)
    for b in range(8):
        inner_tr[b * 256 : (b + 1) * 256, :] = inner_nat[b * 256 : (b + 1) * 256, :].T

    def step(t, carry):
        wait(t)
        a = at_inner(t)
        from_inner(through_inner(a, inner_tr), 4 + t)
        send(4 + t)
        spread_rows(a, STEPS + STEPS - 1 - t)
        wait(8 + t)
        a = at_inner(8 + t)
        from_inner(through_inner(a, inner_nat), 12 + t)
        send(12 + t)
        spread_rows(a, t)
        wait(4 + t)
        put(rows_in, at_outer(4 + t))
        through_outer(outer_tr)
        from_outer(reweight(whole(rows_out), STEPS - 2 - t), t + 1)
        send(t + 1)
        wait(12 + t)
        put(rows_in, reweight(at_outer(12 + t), t))
        through_outer(outer_nat)
        from_outer(whole(rows_out), 9 + t)
        send(9 + t)
        return carry

    lax.fori_loop(0, STEPS - 1, step, 0)

    def term(t):
        for slot in (t, STEPS + t):
            wait_bytes(rows_received.at[slot, pl.ds(0, GROUP - 1)], rows_recv.at[slot])
        ins, outs = rows_received[t].reshape(256, 256), rows_received[STEPS + t].reshape(256, 256)
        return jnp.dot(ins.T, outs, preferred_element_type=F32)

    mixed_grad = term(1) + term(2)
    grad_sent[...] = mixed_grad.reshape(SEQ, 4, 256)

    last = STEPS - 1
    wait(last)
    a = at_inner(last)
    spread_rows(a, STEPS)
    from_inner(through_inner(a, inner_tr), 4 + last)
    send(4 + last)
    wait(8 + last)
    spread_rows(at_inner(8 + last), last)

    grad = (term(0) + term(last)).reshape(SEQ, 4, 256)
    grad_sent[...] = (grad_sent[...] + grad) * (1.0 / 32.0)
    to_row = place * GROUP + share
    for to_seq in mates:
        copy(grad_sent.at[to_seq], grad_out.at[to_row], grad_send, grad_recv, to_seq)
    keep = pltpu.make_async_copy(grad_sent.at[seq], grad_out.at[to_row], grad_own)
    keep.start()

    wait(4 + last)
    put(rows_in, at_outer(4 + last))
    through_outer(outer_tr)

    def fold(k, carry):
        for half in range(2):
            at = pl.ds(pl.multiple_of(k * 256 + half * 128, 128), 128)
            beta_out[:, at] = rows_out[half, pl.ds(k, 4, stride=64), :]
        return carry

    lax.fori_loop(0, 64, fold, 0, unroll=4)

    keep.wait()
    wait_bytes(grad_out.at[pl.ds(0, SEQ - 1)], grad_recv)
    for slot in range(15):
        wait_bytes(sent.at[slot, pl.ds(0, PEERS - 1)], send_sem.at[slot])
    for slot in range(2 * STEPS):
        wait_bytes(rows_sent.at[slot, pl.ds(0, GROUP - 1)], rows_send.at[slot])
    wait_bytes(relay, relay_send)
    for n in range(2):
        wait_bytes(gathered.at[n, pl.ds(0, 15)], gather_send.at[n])
        wait_bytes(gathered.at[n], core_send.at[n])
    wait_bytes(grad_sent.at[pl.ds(0, SEQ - 1)], grad_send)


def local(outer_factor, inner_factor, alpha_start, beta_end, emissions, normalizers):
    vmem, hbm = pl.BlockSpec(memory_space=pltpu.VMEM), pl.BlockSpec(memory_space=pl.ANY)
    dma = pltpu.SemaphoreType.DMA
    return pl.pallas_call(
        kernel,
        out_shape=(jax.ShapeDtypeStruct((4, 64 * 256), F32), jax.ShapeDtypeStruct((64, 4, 256), F32)),
        in_specs=[pl.BlockSpec(memory_space=pltpu.SMEM), hbm, vmem, vmem, vmem, vmem],
        out_specs=(vmem, hbm),
        scratch_shapes=[
            pltpu.VMEM((64 * 256, 256), BF16),
            pltpu.VMEM((64 * 256, 256), BF16),
            pltpu.VMEM((8 * 256, 256), BF16),
            pltpu.VMEM((8 * 256, 256), BF16),
            pltpu.VMEM((GROUP, 32, 256), BF16),
            pltpu.VMEM((4, 32, 256), BF16),
            pltpu.VMEM((4, 16, 32, 256), BF16),
            pltpu.VMEM((15, PEERS, 16, 128), BF16),
            pltpu.VMEM((15, PEERS, 16, 128), BF16),
            pltpu.VMEM((2 * STEPS, GROUP, 32, 256), BF16),
            pltpu.VMEM((2 * STEPS, GROUP, 32, 256), BF16),
            pltpu.VMEM((SEQ, 4, 256), F32),
            pltpu.VMEM((STEPS, 2, 256, 128), F32),
            pltpu.VMEM((2, 256, 128), F32),
            pltpu.VMEM((2, 256, 128), F32),
            pltpu.VMEM((2, 256, 128), F32),
            dma,
            dma((15,)),
            dma((15,)),
            dma,
            dma,
            dma((2,)),
            dma((2,)),
            dma((2,)),
            dma((2,)),
            dma((2 * STEPS,)),
            dma((2 * STEPS,)),
            dma,
            dma,
            dma,
        ],
        compiler_params=pltpu.CompilerParams(
            collective_id=0, has_side_effects=True, vmem_limit_bytes=56 * 1024 * 1024
        ),
    )(
        normalizers,
        outer_factor.reshape(64 * 256, 256),
        inner_factor,
        alpha_start,
        beta_end,
        emissions,
    )


def solution(mesh):
    placed = (
        P("state", None, None),
        P("state", "seq", None),
        P("seq", "state"),
        P("seq", "state"),
        P(None, "seq", "state"),
        P(None, "seq"),
    )
    return jax.shard_map(
        local,
        mesh=mesh,
        in_specs=placed,
        out_specs=(P("seq", "state"), P("state", "seq", None)),
        check_vma=False,
    )
```

```python
import functools

import jax
import jax.numpy as jnp
from jax import lax
from jax.experimental import pallas as pl
from jax.experimental.pallas import tpu as pltpu
from jax.sharding import PartitionSpec as P

MESH = pl.DeviceIdType.MESH
F32, BF16 = jnp.float32, jnp.bfloat16

GROUP = 8
PEERS = 32
SEQ = 64
STEPS = 4


def iota(shape, dim):
    return lax.broadcasted_iota(jnp.int32, shape, dim)


def kernel(
    norm_hbm, outer_hbm, inner_hbm, alpha_hbm, beta_hbm, emis_hbm,
    beta_out, grad_out,
    norm_ref, inner_ref, alpha_ref, beta_ref, emis_ref,
    outer_nat, outer_tr, inner_nat, inner_tr, slab, gathered, sent, received, rows_sent, rows_received,
    grad_sent, emis, rows_in, rows_out, mixed,
    load_sem, send_sem, recv_sem, gather_send, gather_recv, core_send, core_recv,
    rows_send, rows_recv, grad_send, grad_recv, grad_own,
):
    seq, state = lax.axis_index("seq"), lax.axis_index("state")
    x = lax.div(seq, 16)
    y = lax.rem(lax.div(seq, 4), 4)
    low = lax.rem(lax.div(seq, 2), 2)
    core = lax.rem(seq, 2)
    place = y * 2 + low
    share = x * 2 + core
    me = state * GROUP + place

    xs = [lax.rem(x + d, 4) for d in range(4)]
    ys = [lax.rem(y + d, 4) for d in range(4)]
    lows = [low, 1 - low]
    cores = [core, 1 - core]
    opposite = lax.rem(state + 2, 4)
    pairs = [lax.div(opposite, 2), lax.div(state, 2)]

    def mate_of(s):
        return s + 1 - 2 * lax.rem(s, 2)

    orders = [
        [(opposite, 0), (opposite, 1), (mate_of(opposite), 0), (mate_of(opposite), 1)],
        [(mate_of(state), 0), (mate_of(state), 1), (state, 1), (state, 0)],
    ]
    far = (2, 1, 3, 0)
    peers = [
        [
            (to_state * GROUP + ys[dy] * 2 + lows[dl], x * 16 + ys[dy] * 4 + lows[dl] * 2 + core, to_state)
            for to_state, dl in order for dy in far if to_state is not state or dl or dy
        ]
        for order in orders
    ]
    mates = [
        xs[dx] * 16 + ys[dy] * 4 + lows[dl] * 2 + cores[dc]
        for dx in far for dy in far for dl in (1, 0) for dc in (1, 0) if dx or dy or dl or dc
    ]
    sharers = [
        (xs[dx] * 2 + cores[dc], xs[dx] * 16 + y * 4 + low * 2 + cores[dc])
        for dx in far for dc in (1, 0) if dx or dc
    ]
    alike = [
        (dl, ys[dy] * 2 + lows[dl], xs[dx] * 16 + ys[dy] * 4 + lows[dl] * 2 + core)
        for dl in (1, 0) for dx in far for dy in far if dl or dx or dy
    ]
    sibling = x * 16 + y * 4 + low * 2 + 1 - core

    barrier = pltpu.get_barrier_semaphore()
    greeted = 0
    for to_seq, to_state in [p[1:] for p in peers[0] + peers[1] if p[2] is not state] + [(m, state) for m in mates]:
        pl.semaphore_signal(barrier, 1, device_id=(to_seq, to_state), device_id_type=MESH)
        greeted += 1

    pieces = ((inner_hbm, inner_ref), (beta_hbm, beta_ref), (emis_hbm, emis_ref), (norm_hbm, norm_ref),
              (alpha_hbm, alpha_ref), (outer_hbm, outer_nat))
    loads = [pltpu.make_async_copy(src, dst, load_sem.at[i]) for i, (src, dst) in enumerate(pieces)]
    for load in loads:
        load.start()

    def copy(src, dst, send_to, recv_on, to_seq, to_state=state):
        pltpu.make_async_remote_copy(
            src_ref=src, dst_ref=dst, send_sem=send_to, recv_sem=recv_on,
            device_id=(to_seq, to_state), device_id_type=MESH,
        ).start()

    def wait_bytes(ref, sem):
        pltpu.make_async_copy(ref, ref, sem).wait()

    def send(slot, turn):
        for to, to_seq, to_state in peers[turn]:
            copy(sent.at[slot, to], received.at[slot, me], send_sem.at[slot], recv_sem.at[slot], to_seq, to_state)
        if turn == 1:
            received[slot, pl.ds(me, 1)] = sent[slot, pl.ds(me, 1)]

    def wait(slot):
        wait_bytes(received.at[slot, pl.ds(0, PEERS - 1)], recv_sem.at[slot])

    def whole(ref, rows=slice(None)):
        return jnp.concatenate([ref[0, rows, :], ref[1, rows, :]], axis=1)

    def put(ref, a, rows=slice(None)):
        ref[0, rows, :] = a[:, :128]
        ref[1, rows, :] = a[:, 128:]

    low_half = iota((128, 128), 1) < 64

    def swap(a):
        return pltpu.roll(a, 64, 1)

    def at_inner(slot):
        a = [received[slot, s * GROUP : (s + 1) * GROUP].astype(F32).reshape(128, 128) for s in range(4)]
        top = [jnp.where(low_half, a[0], swap(a[1])), jnp.where(low_half, a[2], swap(a[3]))]
        bottom = [jnp.where(low_half, swap(a[0]), a[1]), jnp.where(low_half, swap(a[2]), a[3])]
        return jnp.concatenate([jnp.concatenate(top, axis=1), jnp.concatenate(bottom, axis=1)], axis=0)

    def through_inner(a, factor, slot):
        block = lax.rem(iota((256, 256), 0), 8)
        spread = jnp.concatenate([jnp.where(block == b, a, 0.0).astype(BF16) for b in range(8)], axis=1)
        o = jnp.dot(spread, factor[...], preferred_element_type=F32)
        for u in range(2):
            even, odd = o[:128, u * 128 : (u + 1) * 128], o[128:, u * 128 : (u + 1) * 128]
            first = jnp.where(low_half, even, swap(odd))
            second = jnp.where(low_half, swap(even), odd)
            both = jnp.concatenate([first, second], axis=0).astype(BF16).reshape(2 * GROUP, 16, 128)
            sent[slot, 2 * u * GROUP : (2 * u + 2) * GROUP] = both
        for turn in range(2):
            send(slot, turn)

    def at_outer(slot):
        a = received[slot].astype(F32)
        both = jnp.concatenate([a[:, :8].reshape(256, 128), a[:, 8:].reshape(256, 128)], axis=1)
        return both.T

    def from_outer(a, slot, turn):
        t = a.T.reshape(2 * GROUP, 8, 256)
        both = jnp.concatenate([t[:, :, :128], t[:, :, 128:]], axis=1).astype(BF16)
        sent[slot, pl.ds(pl.multiple_of(pairs[turn] * 2 * GROUP, 2 * GROUP), 2 * GROUP)] = both
        send(slot, turn)

    def through_outer(factor, u):
        half = pl.ds(pl.multiple_of(u * 128, 128), 128)
        block = lax.rem(iota((64, 256), 0), 16)
        for g in range(4):
            part = jnp.concatenate([whole(rows_in, slice(n * 64 + g * 16, n * 64 + g * 16 + 16)) for n in range(4)], axis=0)
            spread = jnp.concatenate([jnp.where(block == b, part, 0.0).astype(BF16) for b in range(16)], axis=1)
            o = jnp.dot(spread, factor[g * 4096 : (g + 1) * 4096, half], preferred_element_type=F32)
            for n in range(4):
                rows_out[u, n * 64 + g * 16 : n * 64 + g * 16 + 16, :] = o[n * 16 : (n + 1) * 16]

    def outer_stage(factor, slot, step=None):
        for turn in range(2):
            u = pairs[turn]
            through_outer(factor, u)
            a = rows_out[u]
            from_outer(a if step is None else a * emis[step, u], slot, turn)

    def unfold(part, dst, scale=None):
        def one(k, carry):
            for half in range(2):
                a = part(pl.ds(pl.multiple_of(k * 256 + half * 128, 128), 128)).astype(F32)
                dst[half, pl.ds(k, 4, stride=64), :] = a if scale is None else a * scale
            return carry

        lax.fori_loop(0, 64, one, 0, unroll=4)

    def unfold_emissions(t):
        row = iota((4, 128), 0)
        norm = jnp.full((4, 128), norm_ref[t, 0], F32)
        for n in range(1, 4):
            norm = jnp.where(row == n, norm_ref[t, n], norm)
        unfold(lambda at: emis_ref[t, :, at], emis.at[t], 1.0 / norm)

    def spread_rows(a, slot):
        put(mixed, a)
        for b in range(GROUP):
            rows_sent[slot, b] = whole(mixed, pl.ds(b, 32, stride=8)).astype(BF16)
        for to, to_seq in sharers:
            copy(rows_sent.at[slot, to], rows_received.at[slot, share], rows_send.at[slot], rows_recv.at[slot], to_seq)
        rows_received[slot, pl.ds(share, 1)] = rows_sent[slot, pl.ds(share, 1)]

    last = STEPS - 1
    loads[0].wait()
    for j in range(64):
        put(mixed, inner_ref[j].astype(F32), slice(j * 4, (j + 1) * 4))
    slab[...] = whole(mixed).astype(BF16).reshape(GROUP, 32, 256)
    pl.semaphore_wait(barrier, greeted)

    own, other = low * 2 + core, (1 - low) * 2 + core
    for dl, to, to_seq in alike:
        copy(slab.at[to], gathered.at[own, x * 4 + y], gather_send.at[dl], gather_recv.at[dl], to_seq)
    gathered[own, pl.ds(x * 4 + y, 1)] = slab[pl.ds(place, 1)]

    for load in loads[1:4]:
        load.wait()
    unfold(lambda at: beta_ref[:, at], rows_out)
    unfold_emissions(last)
    for turn in range(2):
        u = pairs[turn]
        from_outer(rows_out[u] * emis[last, u], 0, turn)

    loads[4].wait()
    unfold(lambda at: alpha_ref[:, at], rows_in)
    loads[5].wait()
    outer_stage(outer_nat, 8)

    def turn_block(k, carry):
        at = pl.ds(pl.multiple_of(k * 256, 256), 256)
        outer_tr[at, :] = outer_nat[at, :].T
        return carry

    wait_bytes(gathered.at[own, pl.ds(0, 15)], gather_recv.at[0])
    copy(gathered.at[own], gathered.at[own], core_send.at[0], core_recv.at[0], sibling)
    lax.fori_loop(0, 16, turn_block, 0)
    wait_bytes(gathered.at[other], gather_recv.at[1])
    copy(gathered.at[other], gathered.at[other], core_send.at[1], core_recv.at[1], sibling)
    lax.fori_loop(16, 64, turn_block, 0)
    for t in range(last):
        unfold_emissions(t)
    wait_bytes(gathered.at[own], core_recv.at[0])
    wait_bytes(gathered.at[other], core_recv.at[1])

    r, c = iota((512, 512), 0), iota((512, 512), 1)
    move = jnp.where(c == r // 4 % 4 * 128 + r // 16 % 4 * 32 + r // 64 * 4 + r % 4, 1.0, 0.0).astype(BF16)
    for q in range(4):
        part = jnp.concatenate([gathered[lc, q * 4 : (q + 1) * 4].reshape(128, 256) for lc in range(4)], axis=0)
        o = jnp.dot(move, part, preferred_element_type=F32)
        for b in range(8):
            inner_nat[b * 256 + q * 64 : b * 256 + (q + 1) * 64, :] = o[b * 64 : (b + 1) * 64].astype(BF16)
    for b in range(8):
        inner_tr[b * 256 : (b + 1) * 256, :] = inner_nat[b * 256 : (b + 1) * 256, :].T

    def step(t, carry):
        wait(t)
        a = at_inner(t)
        through_inner(a, inner_tr, 4 + t)
        spread_rows(a, STEPS + last - t)
        wait(8 + t)
        a = at_inner(8 + t)
        through_inner(a, inner_nat, 12 + t)
        spread_rows(a, t)
        wait(4 + t)
        put(rows_in, at_outer(4 + t))
        outer_stage(outer_tr, t + 1, last - 1 - t)
        wait(12 + t)
        put(rows_in, at_outer(12 + t) * whole(emis.at[t]))
        outer_stage(outer_nat, 9 + t)
        return carry

    lax.fori_loop(0, STEPS - 1, step, 0)

    def term(t):
        for slot in (t, STEPS + t):
            wait_bytes(rows_received.at[slot, pl.ds(0, GROUP - 1)], rows_recv.at[slot])
        ins, outs = rows_received[t].reshape(256, 256), rows_received[STEPS + t].reshape(256, 256)
        return jnp.dot(ins.T, outs, preferred_element_type=F32)

    mixed_grad = term(1) + term(2)
    grad_sent[...] = mixed_grad.reshape(SEQ, 4, 256)

    wait(last)
    a = at_inner(last)
    through_inner(a, inner_tr, 4 + last)
    spread_rows(a, STEPS)
    wait(8 + last)
    spread_rows(at_inner(8 + last), last)

    grad = (term(0) + term(last)).reshape(SEQ, 4, 256)
    grad_sent[...] = (grad_sent[...] + grad) * (1.0 / 32.0)
    to_row = place * GROUP + share
    for to_seq in mates:
        copy(grad_sent.at[to_seq], grad_out.at[to_row], grad_send, grad_recv, to_seq)
    keep = pltpu.make_async_copy(grad_sent.at[seq], grad_out.at[to_row], grad_own)
    keep.start()

    wait(4 + last)
    put(rows_in, at_outer(4 + last))
    for u in range(2):
        through_outer(outer_tr, u)

    def fold(k, carry):
        for half in range(2):
            at = pl.ds(pl.multiple_of(k * 256 + half * 128, 128), 128)
            beta_out[:, at] = rows_out[half, pl.ds(k, 4, stride=64), :]
        return carry

    lax.fori_loop(0, 64, fold, 0, unroll=4)

    keep.wait()
    wait_bytes(grad_out.at[pl.ds(0, SEQ - 1)], grad_recv)
    for slot in range(15):
        wait_bytes(sent.at[slot, pl.ds(0, PEERS - 1)], send_sem.at[slot])
    for slot in range(2 * STEPS):
        wait_bytes(rows_sent.at[slot, pl.ds(0, GROUP - 1)], rows_send.at[slot])
    wait_bytes(gathered.at[0, pl.ds(0, 15)], gather_send.at[0])
    wait_bytes(gathered.at[0], gather_send.at[1])
    for n in range(2):
        wait_bytes(gathered.at[n], core_send.at[n])
    wait_bytes(grad_sent.at[pl.ds(0, SEQ - 1)], grad_send)


def finish(beta, grad, beta_out, grad_out):
    beta_out[...] = beta[...]
    grad_out[...] = grad[...]


def local(outer_factor, inner_factor, alpha_start, beta_end, emissions, normalizers):
    vmem, hbm = pl.BlockSpec(memory_space=pltpu.VMEM), pl.BlockSpec(memory_space=pl.ANY)
    dma = pltpu.SemaphoreType.DMA
    results = (jax.ShapeDtypeStruct((4, 64 * 256), F32), jax.ShapeDtypeStruct((64, 4, 256), F32))
    beta_start, grad = pl.pallas_call(
        kernel,
        out_shape=results,
        in_specs=[hbm] * 6,
        out_specs=(vmem, hbm),
        scratch_shapes=[
            pltpu.SMEM((STEPS, 4), F32),
            pltpu.VMEM((64, 4, 256), BF16),
            pltpu.VMEM((4, 64 * 256), BF16),
            pltpu.VMEM((4, 64 * 256), BF16),
            pltpu.VMEM((STEPS, 4, 64 * 256), BF16),
            pltpu.VMEM((64 * 256, 256), BF16),
            pltpu.VMEM((64 * 256, 256), BF16),
            pltpu.VMEM((8 * 256, 256), BF16),
            pltpu.VMEM((8 * 256, 256), BF16),
            pltpu.VMEM((GROUP, 32, 256), BF16),
            pltpu.VMEM((4, 16, 32, 256), BF16),
            pltpu.VMEM((15, PEERS, 16, 128), BF16),
            pltpu.VMEM((15, PEERS, 16, 128), BF16),
            pltpu.VMEM((2 * STEPS, GROUP, 32, 256), BF16),
            pltpu.VMEM((2 * STEPS, GROUP, 32, 256), BF16),
            pltpu.VMEM((SEQ, 4, 256), F32),
            pltpu.VMEM((STEPS, 2, 256, 128), F32),
            pltpu.VMEM((2, 256, 128), F32),
            pltpu.VMEM((2, 256, 128), F32),
            pltpu.VMEM((2, 256, 128), F32),
            dma((6,)),
            dma((15,)),
            dma((15,)),
            dma((2,)),
            dma((2,)),
            dma((2,)),
            dma((2,)),
            dma((2 * STEPS,)),
            dma((2 * STEPS,)),
            dma,
            dma,
            dma,
        ],
        compiler_params=pltpu.CompilerParams(
            collective_id=0, has_side_effects=True, vmem_limit_bytes=56 * 1024 * 1024
        ),
    )(
        normalizers,
        outer_factor.reshape(64 * 256, 256),
        inner_factor,
        alpha_start,
        beta_end,
        emissions,
    )
    return pl.pallas_call(
        finish,
        out_shape=results,
        in_specs=[vmem, vmem],
        out_specs=(vmem, vmem),
    )(beta_start, grad)


def solution(mesh):
    placed = (
        P("state", None, None),
        P("state", "seq", None),
        P("seq", "state"),
        P("seq", "state"),
        P(None, "seq", "state"),
        P(None, "seq"),
    )
    return jax.shard_map(
        local,
        mesh=mesh,
        in_specs=placed,
        out_specs=(P("seq", "state"), P("state", "seq", None)),
        check_vma=False,
    )
```

```python
import functools

import jax
import jax.numpy as jnp
from jax import lax
from jax.experimental import pallas as pl
from jax.experimental.pallas import tpu as pltpu
from jax.sharding import PartitionSpec as P

MESH = pl.DeviceIdType.MESH
F32, BF16 = jnp.float32, jnp.bfloat16

GROUP = 8
PEERS = 32
SEQ = 64
STEPS = 4


def iota(shape, dim):
    return lax.broadcasted_iota(jnp.int32, shape, dim)


def kernel(
    norm_hbm, outer_hbm, inner_hbm, alpha_hbm, beta_hbm, emis_hbm,
    beta_out, grad_out,
    norm_ref, inner_ref, alpha_ref, beta_ref, emis_ref,
    outer_nat, outer_tr, inner_nat, inner_tr, slab, gathered, sent, received, rows_sent, rows_received,
    grad_sent, emis, rows_in, rows_out, mixed,
    load_sem, send_sem, recv_sem, gather_send, gather_recv, core_send, core_recv,
    rows_send, rows_recv, grad_send, grad_recv, grad_own,
):
    seq, state = lax.axis_index("seq"), lax.axis_index("state")
    x = lax.div(seq, 16)
    y = lax.rem(lax.div(seq, 4), 4)
    low = lax.rem(lax.div(seq, 2), 2)
    core = lax.rem(seq, 2)
    place = y * 2 + low
    share = x * 2 + core
    me = state * GROUP + place

    xs = [lax.rem(x + d, 4) for d in range(4)]
    ys = [lax.rem(y + d, 4) for d in range(4)]
    lows = [low, 1 - low]
    cores = [core, 1 - core]
    opposite = lax.rem(state + 2, 4)
    pairs = [lax.div(opposite, 2), lax.div(state, 2)]

    def mate_of(s):
        return s + 1 - 2 * lax.rem(s, 2)

    orders = [
        [(opposite, 0), (opposite, 1), (mate_of(opposite), 0), (mate_of(opposite), 1)],
        [(mate_of(state), 0), (mate_of(state), 1), (state, 1), (state, 0)],
    ]
    far = (2, 1, 3, 0)
    peers = [
        [
            (to_state * GROUP + ys[dy] * 2 + lows[dl], x * 16 + ys[dy] * 4 + lows[dl] * 2 + core, to_state)
            for to_state, dl in order for dy in far if to_state is not state or dl or dy
        ]
        for order in orders
    ]
    mates = [
        xs[dx] * 16 + ys[dy] * 4 + lows[dl] * 2 + cores[dc]
        for dl in (1, 0) for dx in far for dy in far for dc in (1, 0) if dx or dy or dl or dc
    ]
    sharers = [
        (xs[dx] * 2 + cores[dc], xs[dx] * 16 + y * 4 + low * 2 + cores[dc])
        for dx in far for dc in (1, 0) if dx or dc
    ]
    alike = [
        (dl, ys[dy] * 2 + lows[dl], xs[dx] * 16 + ys[dy] * 4 + lows[dl] * 2 + core)
        for dl in (1, 0) for dx in far for dy in far if dl or dx or dy
    ]
    sibling = x * 16 + y * 4 + low * 2 + 1 - core

    barrier = pltpu.get_barrier_semaphore()
    greeted = 0
    for to_seq, to_state in [p[1:] for p in peers[0] + peers[1] if p[2] is not state] + [(m, state) for m in mates]:
        pl.semaphore_signal(barrier, 1, device_id=(to_seq, to_state), device_id_type=MESH)
        greeted += 1

    pieces = ((inner_hbm, inner_ref), (beta_hbm, beta_ref), (emis_hbm, emis_ref), (norm_hbm, norm_ref),
              (alpha_hbm, alpha_ref), (outer_hbm, outer_nat))
    loads = [pltpu.make_async_copy(src, dst, load_sem.at[i]) for i, (src, dst) in enumerate(pieces)]
    for load in loads:
        load.start()

    def copy(src, dst, send_to, recv_on, to_seq, to_state=state):
        pltpu.make_async_remote_copy(
            src_ref=src, dst_ref=dst, send_sem=send_to, recv_sem=recv_on,
            device_id=(to_seq, to_state), device_id_type=MESH,
        ).start()

    def wait_bytes(ref, sem):
        pltpu.make_async_copy(ref, ref, sem).wait()

    def send(slot, turn):
        for to, to_seq, to_state in peers[turn]:
            copy(sent.at[slot, to], received.at[slot, me], send_sem.at[slot], recv_sem.at[slot], to_seq, to_state)
        if turn == 1:
            received[slot, pl.ds(me, 1)] = sent[slot, pl.ds(me, 1)]

    def wait(slot):
        wait_bytes(received.at[slot, pl.ds(0, PEERS - 1)], recv_sem.at[slot])

    def whole(ref, rows=slice(None)):
        return jnp.concatenate([ref[0, rows, :], ref[1, rows, :]], axis=1)

    def put(ref, a, rows=slice(None)):
        ref[0, rows, :] = a[:, :128]
        ref[1, rows, :] = a[:, 128:]

    low_half = iota((128, 128), 1) < 64

    def swap(a):
        return pltpu.roll(a, 64, 1)

    def at_inner(slot):
        a = [received[slot, s * GROUP : (s + 1) * GROUP].astype(F32).reshape(128, 128) for s in range(4)]
        top = [jnp.where(low_half, a[0], swap(a[1])), jnp.where(low_half, a[2], swap(a[3]))]
        bottom = [jnp.where(low_half, swap(a[0]), a[1]), jnp.where(low_half, swap(a[2]), a[3])]
        return jnp.concatenate([jnp.concatenate(top, axis=1), jnp.concatenate(bottom, axis=1)], axis=0)

    def through_inner(a, factor, slot):
        block = lax.rem(iota((256, 256), 0), 8)
        spread = jnp.concatenate([jnp.where(block == b, a, 0.0).astype(BF16) for b in range(8)], axis=1)
        o = jnp.dot(spread, factor[...], preferred_element_type=F32)
        for u in range(2):
            even, odd = o[:128, u * 128 : (u + 1) * 128], o[128:, u * 128 : (u + 1) * 128]
            first = jnp.where(low_half, even, swap(odd))
            second = jnp.where(low_half, swap(even), odd)
            both = jnp.concatenate([first, second], axis=0).astype(BF16).reshape(2 * GROUP, 16, 128)
            sent[slot, 2 * u * GROUP : (2 * u + 2) * GROUP] = both
        for turn in range(2):
            send(slot, turn)

    def at_outer(slot):
        a = received[slot].astype(F32)
        both = jnp.concatenate([a[:, :8].reshape(256, 128), a[:, 8:].reshape(256, 128)], axis=1)
        return both.T

    def from_outer(a, slot, turn, go=True):
        t = a.T.reshape(2 * GROUP, 8, 256)
        both = jnp.concatenate([t[:, :, :128], t[:, :, 128:]], axis=1).astype(BF16)
        sent[slot, pl.ds(pl.multiple_of(pairs[turn] * 2 * GROUP, 2 * GROUP), 2 * GROUP)] = both
        if go:
            send(slot, turn)

    def through_outer(factor, u):
        half = pl.ds(pl.multiple_of(u * 128, 128), 128)
        block = lax.rem(iota((64, 256), 0), 16)
        for g in range(4):
            part = jnp.concatenate([whole(rows_in, slice(n * 64 + g * 16, n * 64 + g * 16 + 16)) for n in range(4)], axis=0)
            spread = jnp.concatenate([jnp.where(block == b, part, 0.0).astype(BF16) for b in range(16)], axis=1)
            o = jnp.dot(spread, factor[g * 4096 : (g + 1) * 4096, half], preferred_element_type=F32)
            for n in range(4):
                rows_out[u, n * 64 + g * 16 : n * 64 + g * 16 + 16, :] = o[n * 16 : (n + 1) * 16]

    def outer_stage(factor, slot, step=None, go=True):
        for turn in range(2):
            u = pairs[turn]
            through_outer(factor, u)
            a = rows_out[u]
            from_outer(a if step is None else a * emis[step, u], slot, turn, go)

    def unfold(part, dst, scale=None):
        def one(k, carry):
            for half in range(2):
                a = part(pl.ds(pl.multiple_of(k * 256 + half * 128, 128), 128)).astype(F32)
                dst[half, pl.ds(k, 4, stride=64), :] = a if scale is None else a * scale
            return carry

        lax.fori_loop(0, 64, one, 0, unroll=4)

    def unfold_emissions(t):
        row = iota((4, 128), 0)
        norm = jnp.full((4, 128), norm_ref[t, 0], F32)
        for n in range(1, 4):
            norm = jnp.where(row == n, norm_ref[t, n], norm)
        unfold(lambda at: emis_ref[t, :, at], emis.at[t], 1.0 / norm)

    def spread_rows(a, slot):
        put(mixed, a)
        for b in range(GROUP):
            rows_sent[slot, b] = whole(mixed, pl.ds(b, 32, stride=8)).astype(BF16)
        for to, to_seq in sharers:
            copy(rows_sent.at[slot, to], rows_received.at[slot, share], rows_send.at[slot], rows_recv.at[slot], to_seq)
        rows_received[slot, pl.ds(share, 1)] = rows_sent[slot, pl.ds(share, 1)]

    last = STEPS - 1
    loads[0].wait()
    for j in range(64):
        put(mixed, inner_ref[j].astype(F32), slice(j * 4, (j + 1) * 4))
    slab[...] = whole(mixed).astype(BF16).reshape(GROUP, 32, 256)
    for load in loads[1:4]:
        load.wait()
    unfold(lambda at: beta_ref[:, at], rows_out)
    unfold_emissions(last)
    for turn in range(2):
        u = pairs[turn]
        from_outer(rows_out[u] * emis[last, u], 0, turn, go=False)
    loads[4].wait()
    unfold(lambda at: alpha_ref[:, at], rows_in)
    loads[5].wait()
    outer_stage(outer_nat, 8, go=False)
    own, other = low * 2 + core, (1 - low) * 2 + core
    gathered[own, pl.ds(x * 4 + y, 1)] = slab[pl.ds(place, 1)]
    pl.semaphore_wait(barrier, greeted)

    def send_slab(over):
        for dl, to, to_seq in alike:
            if dl == over:
                copy(slab.at[to], gathered.at[own, x * 4 + y], gather_send.at[dl], gather_recv.at[dl], to_seq)

    send_slab(1)
    send(0, 0)
    send(0, 1)
    send_slab(0)
    send(8, 0)
    send(8, 1)

    def turn_block(k, carry):
        at = pl.ds(pl.multiple_of(k * 256, 256), 256)
        outer_tr[at, :] = outer_nat[at, :].T
        return carry

    lax.fori_loop(0, 40, turn_block, 0)
    wait_bytes(gathered.at[own, pl.ds(0, 15)], gather_recv.at[0])
    copy(gathered.at[own], gathered.at[own], core_send.at[0], core_recv.at[0], sibling)
    lax.fori_loop(40, 64, turn_block, 0)
    wait_bytes(gathered.at[other], gather_recv.at[1])
    copy(gathered.at[other], gathered.at[other], core_send.at[1], core_recv.at[1], sibling)
    for t in range(last):
        unfold_emissions(t)
    wait_bytes(gathered.at[own], core_recv.at[0])
    wait_bytes(gathered.at[other], core_recv.at[1])

    r, c = iota((512, 512), 0), iota((512, 512), 1)
    move = jnp.where(c == r // 4 % 4 * 128 + r // 16 % 4 * 32 + r // 64 * 4 + r % 4, 1.0, 0.0).astype(BF16)
    for q in range(4):
        part = jnp.concatenate([gathered[lc, q * 4 : (q + 1) * 4].reshape(128, 256) for lc in range(4)], axis=0)
        o = jnp.dot(move, part, preferred_element_type=F32)
        for b in range(8):
            inner_nat[b * 256 + q * 64 : b * 256 + (q + 1) * 64, :] = o[b * 64 : (b + 1) * 64].astype(BF16)
    for b in range(8):
        inner_tr[b * 256 : (b + 1) * 256, :] = inner_nat[b * 256 : (b + 1) * 256, :].T

    def step(t, carry):
        wait(t)
        a = at_inner(t)
        through_inner(a, inner_tr, 4 + t)
        spread_rows(a, STEPS + last - t)
        wait(8 + t)
        a = at_inner(8 + t)
        through_inner(a, inner_nat, 12 + t)
        spread_rows(a, t)
        wait(4 + t)
        put(rows_in, at_outer(4 + t))
        outer_stage(outer_tr, t + 1, last - 1 - t)
        wait(12 + t)
        put(rows_in, at_outer(12 + t) * whole(emis.at[t]))
        outer_stage(outer_nat, 9 + t)
        return carry

    lax.fori_loop(0, STEPS - 1, step, 0)

    def term(t):
        for slot in (t, STEPS + t):
            wait_bytes(rows_received.at[slot, pl.ds(0, GROUP - 1)], rows_recv.at[slot])
        ins, outs = rows_received[t].reshape(256, 256), rows_received[STEPS + t].reshape(256, 256)
        return jnp.dot(ins.T, outs, preferred_element_type=F32)

    mixed_grad = term(1) + term(2)
    grad_sent[...] = mixed_grad.reshape(SEQ, 4, 256)

    wait(last)
    a = at_inner(last)
    through_inner(a, inner_tr, 4 + last)
    spread_rows(a, STEPS)
    wait(8 + last)
    spread_rows(at_inner(8 + last), last)

    grad = (term(0) + term(last)).reshape(SEQ, 4, 256)
    grad_sent[...] = (grad_sent[...] + grad) * (1.0 / 32.0)
    to_row = place * GROUP + share
    for to_seq in mates:
        copy(grad_sent.at[to_seq], grad_out.at[to_row], grad_send, grad_recv, to_seq)
    keep = pltpu.make_async_copy(grad_sent.at[seq], grad_out.at[to_row], grad_own)
    keep.start()

    for slot in range(15):
        wait_bytes(sent.at[slot, pl.ds(0, PEERS - 1)], send_sem.at[slot])
    for slot in range(2 * STEPS):
        wait_bytes(rows_sent.at[slot, pl.ds(0, GROUP - 1)], rows_send.at[slot])
    wait_bytes(gathered.at[0, pl.ds(0, 15)], gather_send.at[0])
    wait_bytes(gathered.at[0], gather_send.at[1])
    for n in range(2):
        wait_bytes(gathered.at[n], core_send.at[n])

    wait(4 + last)
    put(rows_in, at_outer(4 + last))
    stores = [pltpu.make_async_copy(rows_out.at[u], beta_out.at[u], load_sem.at[u]) for u in range(2)]
    for u in range(2):
        through_outer(outer_tr, u)
        stores[u].start()

    keep.wait()
    wait_bytes(grad_sent.at[pl.ds(0, SEQ - 1)], grad_send)
    wait_bytes(grad_out.at[pl.ds(0, SEQ - 1)], grad_recv)
    for store in stores:
        store.wait()


def finish(beta, grad, beta_out, grad_out):
    def fold(k, carry):
        for half in range(2):
            at = pl.ds(pl.multiple_of(k * 256 + half * 128, 128), 128)
            beta_out[:, at] = beta[half, pl.ds(k, 4, stride=64), :]
        return carry

    lax.fori_loop(0, 64, fold, 0, unroll=8)
    grad_out[...] = grad[...]


def local(outer_factor, inner_factor, alpha_start, beta_end, emissions, normalizers):
    vmem, hbm = pl.BlockSpec(memory_space=pltpu.VMEM), pl.BlockSpec(memory_space=pl.ANY)
    dma = pltpu.SemaphoreType.DMA
    results = (jax.ShapeDtypeStruct((4, 64 * 256), F32), jax.ShapeDtypeStruct((64, 4, 256), F32))
    beta_start, grad = pl.pallas_call(
        kernel,
        out_shape=(jax.ShapeDtypeStruct((2, 256, 128), F32), results[1]),
        in_specs=[hbm] * 6,
        out_specs=(hbm, hbm),
        scratch_shapes=[
            pltpu.SMEM((STEPS, 4), F32),
            pltpu.VMEM((64, 4, 256), BF16),
            pltpu.VMEM((4, 64 * 256), BF16),
            pltpu.VMEM((4, 64 * 256), BF16),
            pltpu.VMEM((STEPS, 4, 64 * 256), BF16),
            pltpu.VMEM((64 * 256, 256), BF16),
            pltpu.VMEM((64 * 256, 256), BF16),
            pltpu.VMEM((8 * 256, 256), BF16),
            pltpu.VMEM((8 * 256, 256), BF16),
            pltpu.VMEM((GROUP, 32, 256), BF16),
            pltpu.VMEM((4, 16, 32, 256), BF16),
            pltpu.VMEM((15, PEERS, 16, 128), BF16),
            pltpu.VMEM((15, PEERS, 16, 128), BF16),
            pltpu.VMEM((2 * STEPS, GROUP, 32, 256), BF16),
            pltpu.VMEM((2 * STEPS, GROUP, 32, 256), BF16),
            pltpu.VMEM((SEQ, 4, 256), F32),
            pltpu.VMEM((STEPS, 2, 256, 128), F32),
            pltpu.VMEM((2, 256, 128), F32),
            pltpu.VMEM((2, 256, 128), F32),
            pltpu.VMEM((2, 256, 128), F32),
            dma((6,)),
            dma((15,)),
            dma((15,)),
            dma((2,)),
            dma((2,)),
            dma((2,)),
            dma((2,)),
            dma((2 * STEPS,)),
            dma((2 * STEPS,)),
            dma,
            dma,
            dma,
        ],
        compiler_params=pltpu.CompilerParams(
            collective_id=0, has_side_effects=True, vmem_limit_bytes=56 * 1024 * 1024
        ),
    )(
        normalizers,
        outer_factor.reshape(64 * 256, 256),
        inner_factor,
        alpha_start,
        beta_end,
        emissions,
    )
    return pl.pallas_call(
        finish,
        out_shape=results,
        in_specs=[vmem, vmem],
        out_specs=(vmem, vmem),
    )(beta_start, grad)


def solution(mesh):
    placed = (
        P("state", None, None),
        P("state", "seq", None),
        P("seq", "state"),
        P("seq", "state"),
        P(None, "seq", "state"),
        P(None, "seq"),
    )
    return jax.shard_map(
        local,
        mesh=mesh,
        in_specs=placed,
        out_specs=(P("seq", "state"), P("state", "seq", None)),
        check_vma=False,
    )
```

```python
import functools

import jax
import jax.numpy as jnp
from jax import lax
from jax.experimental import pallas as pl
from jax.experimental.pallas import tpu as pltpu
from jax.sharding import PartitionSpec as P

MESH = pl.DeviceIdType.MESH
F32, BF16 = jnp.float32, jnp.bfloat16

GROUP = 8
PEERS = 32
SEQ = 64
STEPS = 4


def iota(shape, dim):
    return lax.broadcasted_iota(jnp.int32, shape, dim)


def kernel(
    norm_hbm, outer_hbm, inner_hbm, alpha_hbm, beta_hbm, emis_hbm,
    beta_out, grad_out,
    norm_ref, inner_ref, alpha_ref, beta_ref, emis_ref,
    outer_nat, outer_tr, inner_nat, inner_tr, slab, gathered, sent, received, rows_sent, rows_received,
    grad_early, grad_sent, emis, rows_in, rows_out, mixed,
    load_sem, send_sem, recv_sem, gather_send, gather_recv, core_send, core_recv,
    rows_send, rows_recv, grad_send, grad_recv, grad_own,
):
    seq, state = lax.axis_index("seq"), lax.axis_index("state")
    x = lax.div(seq, 16)
    y = lax.rem(lax.div(seq, 4), 4)
    low = lax.rem(lax.div(seq, 2), 2)
    core = lax.rem(seq, 2)
    place = y * 2 + low
    share = x * 2 + core
    me = state * GROUP + place

    xs = [lax.rem(x + d, 4) for d in range(4)]
    ys = [lax.rem(y + d, 4) for d in range(4)]
    lows = [low, 1 - low]
    cores = [core, 1 - core]
    opposite = lax.rem(state + 2, 4)
    pairs = [lax.div(opposite, 2), lax.div(state, 2)]

    def mate_of(s):
        return s + 1 - 2 * lax.rem(s, 2)

    orders = [
        [(opposite, 0), (opposite, 1), (mate_of(opposite), 0), (mate_of(opposite), 1)],
        [(mate_of(state), 0), (mate_of(state), 1), (state, 1), (state, 0)],
    ]
    far = (2, 1, 3, 0)
    peers = [
        [
            (to_state * GROUP + ys[dy] * 2 + lows[dl], x * 16 + ys[dy] * 4 + lows[dl] * 2 + core, to_state)
            for to_state, dl in order for dy in far if to_state is not state or dl or dy
        ]
        for order in orders
    ]
    mates = [
        xs[dx] * 16 + ys[dy] * 4 + lows[dl] * 2 + cores[dc]
        for dl in (1, 0) for dx in far for dy in far for dc in (1, 0) if dx or dy or dl or dc
    ]
    sharers = [
        (xs[dx] * 2 + cores[dc], xs[dx] * 16 + y * 4 + low * 2 + cores[dc])
        for dx in far for dc in (1, 0) if dx or dc
    ]
    alike = [
        (dl, ys[dy] * 2 + lows[dl], xs[dx] * 16 + ys[dy] * 4 + lows[dl] * 2 + core)
        for dl in (1, 0) for dx in far for dy in far if dl or dx or dy
    ]
    sibling = x * 16 + y * 4 + low * 2 + 1 - core

    barrier = pltpu.get_barrier_semaphore()
    greeted = 0
    for to_seq, to_state in [p[1:] for p in peers[0] + peers[1] if p[2] is not state] + [(m, state) for m in mates]:
        pl.semaphore_signal(barrier, 1, device_id=(to_seq, to_state), device_id_type=MESH)
        greeted += 1

    pieces = ((inner_hbm, inner_ref), (beta_hbm, beta_ref), (emis_hbm, emis_ref), (norm_hbm, norm_ref),
              (alpha_hbm, alpha_ref), (outer_hbm, outer_nat))
    loads = [pltpu.make_async_copy(src, dst, load_sem.at[i]) for i, (src, dst) in enumerate(pieces)]
    for load in loads:
        load.start()

    def copy(src, dst, send_to, recv_on, to_seq, to_state=state):
        pltpu.make_async_remote_copy(
            src_ref=src, dst_ref=dst, send_sem=send_to, recv_sem=recv_on,
            device_id=(to_seq, to_state), device_id_type=MESH,
        ).start()

    def wait_bytes(ref, sem):
        pltpu.make_async_copy(ref, ref, sem).wait()

    def send(slot, turn):
        for to, to_seq, to_state in peers[turn]:
            copy(sent.at[slot, to], received.at[slot, me], send_sem.at[slot], recv_sem.at[slot], to_seq, to_state)
        if turn == 1:
            received[slot, pl.ds(me, 1)] = sent[slot, pl.ds(me, 1)]

    def wait(slot):
        wait_bytes(received.at[slot, pl.ds(0, PEERS - 1)], recv_sem.at[slot])

    def whole(ref, rows=slice(None)):
        return jnp.concatenate([ref[0, rows, :], ref[1, rows, :]], axis=1)

    def put(ref, a, rows=slice(None)):
        ref[0, rows, :] = a[:, :128]
        ref[1, rows, :] = a[:, 128:]

    low_half = iota((128, 128), 1) < 64

    def swap(a):
        return pltpu.roll(a, 64, 1)

    def at_inner(slot):
        a = [received[slot, s * GROUP : (s + 1) * GROUP].astype(F32).reshape(128, 128) for s in range(4)]
        top = [jnp.where(low_half, a[0], swap(a[1])), jnp.where(low_half, a[2], swap(a[3]))]
        bottom = [jnp.where(low_half, swap(a[0]), a[1]), jnp.where(low_half, swap(a[2]), a[3])]
        return jnp.concatenate([jnp.concatenate(top, axis=1), jnp.concatenate(bottom, axis=1)], axis=0)

    def through_inner(a, factor, slot):
        block = lax.rem(iota((256, 256), 0), 8)
        spread = jnp.concatenate([jnp.where(block == b, a, 0.0).astype(BF16) for b in range(8)], axis=1)
        o = jnp.dot(spread, factor[...], preferred_element_type=F32)
        for u in range(2):
            even, odd = o[:128, u * 128 : (u + 1) * 128], o[128:, u * 128 : (u + 1) * 128]
            first = jnp.where(low_half, even, swap(odd))
            second = jnp.where(low_half, swap(even), odd)
            both = jnp.concatenate([first, second], axis=0).astype(BF16).reshape(2 * GROUP, 16, 128)
            sent[slot, 2 * u * GROUP : (2 * u + 2) * GROUP] = both
        for turn in range(2):
            send(slot, turn)

    def at_outer(slot):
        a = received[slot].astype(F32)
        both = jnp.concatenate([a[:, :8].reshape(256, 128), a[:, 8:].reshape(256, 128)], axis=1)
        return both.T

    def from_outer(a, slot, turn, go=True):
        t = a.T.reshape(2 * GROUP, 8, 256)
        both = jnp.concatenate([t[:, :, :128], t[:, :, 128:]], axis=1).astype(BF16)
        sent[slot, pl.ds(pl.multiple_of(pairs[turn] * 2 * GROUP, 2 * GROUP), 2 * GROUP)] = both
        if go:
            send(slot, turn)

    def through_outer(factor, u):
        half = pl.ds(pl.multiple_of(u * 128, 128), 128)
        block = lax.rem(iota((64, 256), 0), 16)
        for g in range(4):
            part = jnp.concatenate([whole(rows_in, slice(n * 64 + g * 16, n * 64 + g * 16 + 16)) for n in range(4)], axis=0)
            spread = jnp.concatenate([jnp.where(block == b, part, 0.0).astype(BF16) for b in range(16)], axis=1)
            o = jnp.dot(spread, factor[g * 4096 : (g + 1) * 4096, half], preferred_element_type=F32)
            for n in range(4):
                rows_out[u, n * 64 + g * 16 : n * 64 + g * 16 + 16, :] = o[n * 16 : (n + 1) * 16]

    def outer_stage(factor, slot, step=None, go=True):
        for turn in range(2):
            u = pairs[turn]
            through_outer(factor, u)
            a = rows_out[u]
            from_outer(a if step is None else a * emis[step, u], slot, turn, go)

    def unfold(part, dst, scale=None):
        def one(k, carry):
            for half in range(2):
                a = part(pl.ds(pl.multiple_of(k * 256 + half * 128, 128), 128)).astype(F32)
                dst[half, pl.ds(k, 4, stride=64), :] = a if scale is None else a * scale
            return carry

        lax.fori_loop(0, 64, one, 0, unroll=4)

    def unfold_emissions(t):
        row = iota((4, 128), 0)
        norm = jnp.full((4, 128), norm_ref[t, 0], F32)
        for n in range(1, 4):
            norm = jnp.where(row == n, norm_ref[t, n], norm)
        unfold(lambda at: emis_ref[t, :, at], emis.at[t], 1.0 / norm)

    def spread_rows(a, slot):
        put(mixed, a)
        for b in range(GROUP):
            rows_sent[slot, b] = whole(mixed, pl.ds(b, 32, stride=8)).astype(BF16)
        for to, to_seq in sharers:
            copy(rows_sent.at[slot, to], rows_received.at[slot, share], rows_send.at[slot], rows_recv.at[slot], to_seq)
        rows_received[slot, pl.ds(share, 1)] = rows_sent[slot, pl.ds(share, 1)]

    last = STEPS - 1
    loads[0].wait()
    for j in range(64):
        put(mixed, inner_ref[j].astype(F32), slice(j * 4, (j + 1) * 4))
    slab[...] = whole(mixed).astype(BF16).reshape(GROUP, 32, 256)
    for load in loads[1:4]:
        load.wait()
    unfold(lambda at: beta_ref[:, at], rows_out)
    unfold_emissions(last)
    for turn in range(2):
        u = pairs[turn]
        from_outer(rows_out[u] * emis[last, u], 0, turn, go=False)
    loads[4].wait()
    unfold(lambda at: alpha_ref[:, at], rows_in)
    loads[5].wait()
    outer_stage(outer_nat, 8, go=False)
    own, other = low * 2 + core, (1 - low) * 2 + core
    gathered[own, pl.ds(x * 4 + y, 1)] = slab[pl.ds(place, 1)]
    pl.semaphore_wait(barrier, greeted)

    def send_slab(over):
        for dl, to, to_seq in alike:
            if dl == over:
                copy(slab.at[to], gathered.at[own, x * 4 + y], gather_send.at[dl], gather_recv.at[dl], to_seq)

    send_slab(1)
    send(0, 0)
    send(0, 1)
    send_slab(0)
    send(8, 0)
    send(8, 1)

    def turn_block(k, carry):
        at = pl.ds(pl.multiple_of(k * 256, 256), 256)
        outer_tr[at, :] = outer_nat[at, :].T
        return carry

    lax.fori_loop(0, 40, turn_block, 0)
    wait_bytes(gathered.at[own, pl.ds(0, 15)], gather_recv.at[0])
    copy(gathered.at[own], gathered.at[own], core_send.at[0], core_recv.at[0], sibling)
    lax.fori_loop(40, 64, turn_block, 0)
    wait_bytes(gathered.at[other], gather_recv.at[1])
    copy(gathered.at[other], gathered.at[other], core_send.at[1], core_recv.at[1], sibling)
    for t in range(last):
        unfold_emissions(t)
    wait_bytes(gathered.at[own], core_recv.at[0])
    wait_bytes(gathered.at[other], core_recv.at[1])

    r, c = iota((512, 512), 0), iota((512, 512), 1)
    move = jnp.where(c == r // 4 % 4 * 128 + r // 16 % 4 * 32 + r // 64 * 4 + r % 4, 1.0, 0.0).astype(BF16)
    for q in range(4):
        part = jnp.concatenate([gathered[lc, q * 4 : (q + 1) * 4].reshape(128, 256) for lc in range(4)], axis=0)
        o = jnp.dot(move, part, preferred_element_type=F32)
        for b in range(8):
            inner_nat[b * 256 + q * 64 : b * 256 + (q + 1) * 64, :] = o[b * 64 : (b + 1) * 64].astype(BF16)
    for b in range(8):
        inner_tr[b * 256 : (b + 1) * 256, :] = inner_nat[b * 256 : (b + 1) * 256, :].T

    def step(t, carry):
        wait(t)
        a = at_inner(t)
        through_inner(a, inner_tr, 4 + t)
        spread_rows(a, STEPS + last - t)
        wait(8 + t)
        a = at_inner(8 + t)
        through_inner(a, inner_nat, 12 + t)
        spread_rows(a, t)
        wait(4 + t)
        put(rows_in, at_outer(4 + t))
        outer_stage(outer_tr, t + 1, last - 1 - t)
        wait(12 + t)
        put(rows_in, at_outer(12 + t) * whole(emis.at[t]))
        outer_stage(outer_nat, 9 + t)
        return carry

    lax.fori_loop(0, STEPS - 1, step, 0)

    def term(t):
        for slot in (t, STEPS + t):
            wait_bytes(rows_received.at[slot, pl.ds(0, GROUP - 1)], rows_recv.at[slot])
        ins, outs = rows_received[t].reshape(256, 256), rows_received[STEPS + t].reshape(256, 256)
        return jnp.dot(ins.T, outs, preferred_element_type=F32)

    mixed_grad = term(1) + term(2)
    grad_early[...] = mixed_grad.reshape(SEQ, 4, 256)

    wait(last)
    a = at_inner(last)
    spread_rows(a, STEPS)
    through_inner(a, inner_tr, 4 + last)
    wait(8 + last)
    spread_rows(at_inner(8 + last), last)

    grad = (term(0) + term(last)).reshape(SEQ, 4, 256)
    grad_sent[...] = ((grad_early[...] + grad) * (1.0 / 32.0)).astype(BF16)
    to_row = place * GROUP + share
    for to_seq in mates:
        copy(grad_sent.at[to_seq], grad_out.at[to_row], grad_send, grad_recv, to_seq)
    keep = pltpu.make_async_copy(grad_sent.at[seq], grad_out.at[to_row], grad_own)
    keep.start()

    for slot in range(15):
        wait_bytes(sent.at[slot, pl.ds(0, PEERS - 1)], send_sem.at[slot])
    for slot in range(2 * STEPS):
        wait_bytes(rows_sent.at[slot, pl.ds(0, GROUP - 1)], rows_send.at[slot])
    wait_bytes(gathered.at[0, pl.ds(0, 15)], gather_send.at[0])
    wait_bytes(gathered.at[0], gather_send.at[1])
    for n in range(2):
        wait_bytes(gathered.at[n], core_send.at[n])

    wait(4 + last)
    put(rows_in, at_outer(4 + last))
    stores = [pltpu.make_async_copy(rows_out.at[u], beta_out.at[u], load_sem.at[u]) for u in range(2)]
    for u in range(2):
        through_outer(outer_tr, u)
        stores[u].start()

    keep.wait()
    wait_bytes(grad_sent.at[pl.ds(0, SEQ - 1)], grad_send)
    wait_bytes(grad_out.at[pl.ds(0, SEQ - 1)], grad_recv)
    for store in stores:
        store.wait()


def finish(beta, grad, beta_out, grad_out):
    def fold(k, carry):
        for half in range(2):
            at = pl.ds(pl.multiple_of(k * 256 + half * 128, 128), 128)
            beta_out[:, at] = beta[half, pl.ds(k, 4, stride=64), :]
        return carry

    lax.fori_loop(0, 64, fold, 0, unroll=8)
    grad_out[...] = grad[...].astype(F32)


def local(outer_factor, inner_factor, alpha_start, beta_end, emissions, normalizers):
    vmem, hbm = pl.BlockSpec(memory_space=pltpu.VMEM), pl.BlockSpec(memory_space=pl.ANY)
    dma = pltpu.SemaphoreType.DMA
    results = (jax.ShapeDtypeStruct((4, 64 * 256), F32), jax.ShapeDtypeStruct((64, 4, 256), F32))
    beta_start, grad = pl.pallas_call(
        kernel,
        out_shape=(jax.ShapeDtypeStruct((2, 256, 128), F32), jax.ShapeDtypeStruct((64, 4, 256), BF16)),
        in_specs=[hbm] * 6,
        out_specs=(hbm, hbm),
        scratch_shapes=[
            pltpu.SMEM((STEPS, 4), F32),
            pltpu.VMEM((64, 4, 256), BF16),
            pltpu.VMEM((4, 64 * 256), BF16),
            pltpu.VMEM((4, 64 * 256), BF16),
            pltpu.VMEM((STEPS, 4, 64 * 256), BF16),
            pltpu.VMEM((64 * 256, 256), BF16),
            pltpu.VMEM((64 * 256, 256), BF16),
            pltpu.VMEM((8 * 256, 256), BF16),
            pltpu.VMEM((8 * 256, 256), BF16),
            pltpu.VMEM((GROUP, 32, 256), BF16),
            pltpu.VMEM((4, 16, 32, 256), BF16),
            pltpu.VMEM((15, PEERS, 16, 128), BF16),
            pltpu.VMEM((15, PEERS, 16, 128), BF16),
            pltpu.VMEM((2 * STEPS, GROUP, 32, 256), BF16),
            pltpu.VMEM((2 * STEPS, GROUP, 32, 256), BF16),
            pltpu.VMEM((SEQ, 4, 256), F32),
            pltpu.VMEM((SEQ, 4, 256), BF16),
            pltpu.VMEM((STEPS, 2, 256, 128), F32),
            pltpu.VMEM((2, 256, 128), F32),
            pltpu.VMEM((2, 256, 128), F32),
            pltpu.VMEM((2, 256, 128), F32),
            dma((6,)),
            dma((15,)),
            dma((15,)),
            dma((2,)),
            dma((2,)),
            dma((2,)),
            dma((2,)),
            dma((2 * STEPS,)),
            dma((2 * STEPS,)),
            dma,
            dma,
            dma,
        ],
        compiler_params=pltpu.CompilerParams(
            collective_id=0, has_side_effects=True, vmem_limit_bytes=56 * 1024 * 1024
        ),
    )(
        normalizers,
        outer_factor.reshape(64 * 256, 256),
        inner_factor,
        alpha_start,
        beta_end,
        emissions,
    )
    return pl.pallas_call(
        finish,
        out_shape=results,
        in_specs=[vmem, vmem],
        out_specs=(vmem, vmem),
    )(beta_start, grad)


def solution(mesh):
    placed = (
        P("state", None, None),
        P("state", "seq", None),
        P("seq", "state"),
        P("seq", "state"),
        P(None, "seq", "state"),
        P(None, "seq"),
    )
    return jax.shard_map(
        local,
        mesh=mesh,
        in_specs=placed,
        out_specs=(P("seq", "state"), P("state", "seq", None)),
        check_vma=False,
    )
```
